256 devices in a mesh: rep: 32 (over z_hi, x, core), fsdp: 8 (over z_lo, y).
Axes of the slice: x: 4, y: 4, z: 8 (z_hi: 4, z_lo: 2; z = z_hi * 2 + z_lo), core: 2. Of those that a mesh axis runs over, the one named last changes fastest.
Arguments:
- activations: bfloat16 [131072, 4096], P(('rep', 'fsdp')), may hold values from -6 to 6
- target: bfloat16 [131072, 512], P(('rep', 'fsdp')), may hold values from -6 to 6
- params: float32 [32, 4096, 512], P('rep', 'fsdp'), may hold values from -6 to 6
- momentum: float32 [32, 4096, 512], P('rep', 'fsdp'), may hold values from -6 to 6
- outer_params: float32 [4096, 512], P('fsdp'), may hold values from -6 to 6
- outer_momentum: float32 [4096, 512], P('fsdp'), may hold values from -6 to 6
- pending: float32 [1024, 512], P('fsdp'), may hold values from -6 to 6
- plan: int32 [4], replicated, may hold values from 0 to 3, each once
Outputs:
- new_params: float32 [32, 4096, 512], P('rep', 'fsdp')
- new_momentum: float32 [32, 4096, 512], P('rep', 'fsdp')
- grad_input: bfloat16 [131072, 4096], P(('rep', 'fsdp'))
- new_outer: float32 [4096, 512], P('fsdp')
- new_outer_momentum: float32 [4096, 512], P('fsdp')
- new_pending: float32 [1024, 512], P('fsdp')
The draws below stay inside these ranges and needn't reach their ends.
Inputs may be any that keep to these rules, and one draw needn't show every extreme that they name: plan lists the 4 fragments in the order in which this round synchronizes them, each once.
All inputs are finite; a program needn't handle non-finite values.
Results may differ from the reference program's by a relative error of at most 0.018.
Values may be sent and summed in bfloat16 or wider, within the bound.
No kernel may reach another device: no remote copies, remote signals or barrier semaphores. Data moves between devices by JAX's collectives and lax.ppermute only.
A program may use at most 128 MiB of HBM per device.

```python
import jax
import jax.numpy as jnp
from jax import lax

DW = 4096
HV = 512
TOK_DEV = 512
NFRAG = 4
TOKENS = 131072
REPLICAS = 32
FRAG_ROWS = 128
N_REP = 32
N_FSDP = 8


def block_levels(stream_key, shape, cuts, least, largest):
    gain, own = 1.0, jax.random.fold_in(stream_key, 6)
    for position, shards_of in cuts:
        steps = jnp.exp(jax.random.uniform(jax.random.fold_in(own, position), (shards_of,), jnp.float32, least / len(cuts), largest / len(cuts)))
        gain = gain * jnp.repeat(steps, shape[position] // shards_of).reshape([-1 if axis == position else 1 for axis in range(len(shape))])
    return gain


def normal_values(key, shape, deviation, most, shards=(), dtype=jnp.bfloat16):
    entries = deviation * jax.random.normal(key, shape, jnp.float32)
    if shards:
        entries = entries * block_levels(key, shape, shards, -0.22, 0.18)
    return jnp.clip(entries, -most, most).astype(dtype)


def setup_inputs(seed: int = 0) -> dict:
    key_list = jax.random.split(jax.random.key(seed), 9)
    activations = normal_values(key_list[0], (TOKENS, DW), 1.0, 6.0, ((0, 256),))
    target = normal_values(key_list[1], (TOKENS, HV), 1.0, 6.0, ((0, 256),))
    params = normal_values(key_list[2], (REPLICAS, DW, HV), 1.0, 6.0, ((0, 32), (1, 8)), jnp.float32)
    momentum = normal_values(key_list[3], (REPLICAS, DW, HV), 1.0, 6.0, ((0, 32), (1, 8)), jnp.float32)
    outer_params = normal_values(key_list[4], (DW, HV), 1.0, 6.0, ((0, 8),), jnp.float32)
    outer_momentum = normal_values(key_list[5], (DW, HV), 1.0, 6.0, ((0, 8),), jnp.float32)
    pending = normal_values(key_list[6], (DW // NFRAG, HV), 1.0, 6.0, ((0, 8),), jnp.float32)
    plan = jax.random.permutation(key_list[7], NFRAG).astype(jnp.int32)
    return dict(activations=activations, target=target, params=params, momentum=momentum, outer_params=outer_params, outer_momentum=outer_momentum, pending=pending, plan=plan)


INNER_RATE = 0.05
INNER_BETA = 0.9
OUTER_RATE = 0.7
OUTER_BETA = 0.9
MIX_SHARE = 0.5


def replica_inner(operands):
    tokens_in, targets, weights, moment = operands
    multiplier = DW ** -0.5
    weights16 = weights.astype(jnp.bfloat16)
    values = jnp.dot(tokens_in, weights16, preferred_element_type=jnp.float32) * multiplier
    cotangent = (values - targets.astype(jnp.float32)).astype(jnp.bfloat16)
    grad_input = (jnp.dot(cotangent, weights16.T, preferred_element_type=jnp.float32) * multiplier).astype(jnp.bfloat16)
    blocks = tokens_in.reshape(N_FSDP, TOK_DEV, DW).astype(jnp.float32)
    cot_blocks = cotangent.reshape(N_FSDP, TOK_DEV, HV).astype(jnp.float32)
    partials = jnp.einsum("ntd,nth->ndh", blocks, cot_blocks).astype(jnp.bfloat16)
    partials = lax.optimization_barrier(partials)
    gradient = jnp.sum(partials.astype(jnp.float32), axis=0) * multiplier
    new_moment = INNER_BETA * moment + gradient
    stepped = weights - INNER_RATE * new_moment
    return grad_input, new_moment, stepped


def fragment_rows(matrix, frag_index):
    shaped = matrix.reshape(N_FSDP, NFRAG, FRAG_ROWS, HV)
    chosen = lax.dynamic_index_in_dim(shaped, frag_index, 1, keepdims=False)
    return chosen.reshape(N_FSDP * FRAG_ROWS, HV)


def replace_rows(matrix, frag_index, new_rows):
    shaped = matrix.reshape(N_FSDP, NFRAG, FRAG_ROWS, HV)
    updated = new_rows.reshape(N_FSDP, 1, FRAG_ROWS, HV)
    return lax.dynamic_update_slice_in_dim(shaped, updated, frag_index, 1).reshape(DW, HV)


def reference(activations, target, params, momentum, outer_params, outer_momentum, pending, plan):
    tokens_all = activations.reshape(N_REP, TOK_DEV * N_FSDP, DW)
    targets_all = target.reshape(N_REP, TOK_DEV * N_FSDP, HV)
    grad_input, new_momentum, stepped = lax.map(replica_inner, (tokens_all, targets_all, params, momentum))
    grad_input = grad_input.reshape(TOKENS, DW)
    current = plan[2]
    arrived = plan[0]
    outer_now = fragment_rows(outer_params, current)

    def take_current(matrix):
        return fragment_rows(matrix, current)

    replica_rows = jax.vmap(take_current)(params)
    new_pending = jnp.sum(outer_now[None] - replica_rows, axis=0) / N_REP
    moment_late = OUTER_BETA * fragment_rows(outer_momentum, arrived) + pending
    outer_late = fragment_rows(outer_params, arrived) - OUTER_RATE * (pending + OUTER_BETA * moment_late)
    new_outer_momentum = replace_rows(outer_momentum, arrived, moment_late)
    new_outer = replace_rows(outer_params, arrived, outer_late)

    def merge_replica(matrix):
        return replace_rows(matrix, arrived, MIX_SHARE * fragment_rows(matrix, arrived) + MIX_SHARE * outer_late)

    new_params = jax.vmap(merge_replica)(stepped)
    return new_params, new_momentum, grad_input, new_outer, new_outer_momentum, new_pending
```

```python
import functools

import jax
import jax.numpy as jnp
from jax import lax
from jax.experimental import pallas as pl
from jax.experimental.pallas import tpu as pltpu
from jax.sharding import PartitionSpec as P

DW = 4096
HV = 512
SLAB = 512
TOK = 512
NFRAG = 4
FRAG = SLAB // NFRAG
RA = 288
RB = SLAB - RA
HA = RA // 2
LO = SLAB // 2
ORDER = (6, 5, 7, 2, 4, 1, 3, 0)
FIRST, SECOND, THIRD = (7, 5, 6, 4), (3, 1, 2), (0,)

INNER_RATE = 0.05
INNER_BETA = 0.9
OUTER_RATE = 0.7
OUTER_BETA = 0.9
MIX_SHARE = 0.5
SCALE = DW ** (-0.5)

F32 = jnp.float32
BF16 = jnp.bfloat16
MIB = 1024 * 1024
BIG = 56 * MIB


def move_y(value, step):
    pairs = [(z * 4 + y, z * 4 + (y + step) % 4) for z in range(2) for y in range(4)]
    return lax.ppermute(value, "fsdp", pairs)


def move_z(value):
    return lax.ppermute(value, "fsdp", [(i, (i + 4) % 8) for i in range(8)])


def add16(*terms):
    total = terms[0].astype(F32)
    for term in terms[1:]:
        total = total + term.astype(F32)
    return total


def swap_core(value):
    return lax.ppermute(value, "rep", [(i, i ^ 1) for i in range(32)])


def swap_x(value, flip):
    pairs = []
    for i in range(32):
        x = (i // 2) % 4
        pairs.append((i, i + 2 * ((x ^ flip) - x)))
    return lax.ppermute(value, "rep", pairs)


def swap_z(value, flip):
    pairs = []
    for i in range(32):
        h = i // 8
        pairs.append((i, i + 8 * ((h ^ flip) - h)))
    return lax.ppermute(value, "rep", pairs)


def add_rounded(*terms):
    return add16(*terms).astype(BF16)


def params_of(limit):
    return pltpu.CompilerParams(vmem_limit_bytes=limit)


def turn_kernel(place, x_ref, out_ref):
    out_ref[0] = x_ref[...].T


def turn(place, activations):
    return pl.pallas_call(
        turn_kernel,
        out_shape=jax.ShapeDtypeStruct((8, SLAB, TOK), BF16),
        grid_spec=pltpu.PrefetchScalarGridSpec(
            num_scalar_prefetch=1,
            grid=(8,),
            in_specs=[pl.BlockSpec((TOK, SLAB), lambda d, place: (0, place[d]))],
            out_specs=pl.BlockSpec((1, SLAB, TOK), lambda d, place: (d, 0, 0)),
        ),
        compiler_params=params_of(BIG),
        cost_estimate=pl.CostEstimate(flops=0, bytes_accessed=8 * MIB, transcendentals=0),
    )(place, activations)


def whole(shape):
    return pl.BlockSpec(shape, lambda i, place: (0,) * len(shape))


def forward_kernel(layout, first, last, place, *refs):
    n = len(layout)
    refs = list(refs)
    slabs = [refs.pop(0) for _ in range(n)]
    pieces = [[refs.pop(0) for _ in rows] for rows in layout]
    before = None if first else refs.pop(0)
    target = refs.pop(0) if last else None
    out, weights = refs
    total = None if first else before[...]
    for j in range(n):
        at = 0
        for piece, rows in zip(pieces[j], layout[j]):
            weights[j, at : at + rows, :] = piece[...]
            at += rows
        term = jnp.dot(slabs[j][...], weights[j], preferred_element_type=F32)
        total = term if total is None else total + term
    if last:
        total = (total * SCALE - target[...].astype(F32)).astype(BF16)
    out[...] = total


def forward(place, shards, activations, pieces, before=None, target=None):
    layout = [[p.shape[0] for p in group] for group in pieces]
    n = len(shards)
    slab_specs = [
        pl.BlockSpec((TOK, SLAB), functools.partial(lambda d, i, place: (0, place[d]), d)) for d in shards
    ]
    operands = [p for group in pieces for p in group]
    if before is not None:
        operands.append(before)
    if target is not None:
        operands.append(target)
    out_type = BF16 if target is not None else F32
    return pl.pallas_call(
        functools.partial(forward_kernel, layout, before is None, target is not None),
        out_shape=(
            jax.ShapeDtypeStruct((TOK, HV), out_type),
            jax.ShapeDtypeStruct((n, SLAB, HV), BF16),
        ),
        grid_spec=pltpu.PrefetchScalarGridSpec(
            num_scalar_prefetch=1,
            grid=(1,),
            in_specs=slab_specs + [whole(o.shape) for o in operands],
            out_specs=(whole((TOK, HV)), whole((n, SLAB, HV))),
        ),
        compiler_params=params_of(BIG),
        cost_estimate=pl.CostEstimate(
            flops=2 * n * TOK * SLAB * HV, bytes_accessed=(n + 1) * MIB, transcendentals=0
        ),
    )(place, *([activations] * n), *operands)


def backward_kernel(cuts, turned, cotangent, *outs):
    outs = list(outs)
    for j, rows in enumerate(cuts):
        part = jnp.dot(turned[j], cotangent[...], preferred_element_type=F32).astype(BF16)
        at = 0
        for size in rows:
            outs.pop(0)[...] = part[at : at + size]
            at += size


def backward(turned, cotangent, start, cuts):
    n = len(cuts)
    shapes = [(size, HV) for rows in cuts for size in rows]
    return pl.pallas_call(
        functools.partial(backward_kernel, cuts),
        out_shape=tuple(jax.ShapeDtypeStruct(s, BF16) for s in shapes),
        grid=(1,),
        in_specs=[
            pl.BlockSpec((n, SLAB, TOK), lambda i: (start // n, 0, 0)),
            pl.BlockSpec((TOK, HV), lambda i: (0, 0)),
        ],
        out_specs=tuple(pl.BlockSpec(s, lambda i: (0, 0)) for s in shapes),
        compiler_params=params_of(BIG),
        cost_estimate=pl.CostEstimate(
            flops=2 * n * TOK * SLAB * HV, bytes_accessed=n * MIB, transcendentals=0
        ),
    )(turned, cotangent)


def input_kernel(place, cot, first, second, third, out):
    d = pl.program_id(0)

    def write(weights):
        product = lax.dot_general(
            cot[...], weights[0], (((1,), (1,)), ((), ())), preferred_element_type=F32
        )
        out[...] = (product * SCALE).astype(BF16)

    pl.when(d < 4)(lambda: write(first))
    pl.when((d >= 4) & (d < 7))(lambda: write(second))
    pl.when(d >= 7)(lambda: write(third))


def input_gradient(place, cotangent, first, second, third):
    order = jnp.take(place, jnp.array(FIRST + SECOND + THIRD, jnp.int32))
    return pl.pallas_call(
        input_kernel,
        out_shape=jax.ShapeDtypeStruct((TOK, DW), BF16),
        grid_spec=pltpu.PrefetchScalarGridSpec(
            num_scalar_prefetch=1,
            grid=(8,),
            in_specs=[
                pl.BlockSpec((TOK, HV), lambda d, place: (0, 0)),
                pl.BlockSpec((1, SLAB, HV), lambda d, place: (jnp.minimum(d, 3), 0, 0)),
                pl.BlockSpec((1, SLAB, HV), lambda d, place: (jnp.clip(d - 4, 0, 2), 0, 0)),
                pl.BlockSpec((1, SLAB, HV), lambda d, place: (0, 0, 0)),
            ],
            out_specs=pl.BlockSpec((TOK, SLAB), lambda d, place: (0, place[d])),
        ),
        compiler_params=params_of(BIG),
        cost_estimate=pl.CostEstimate(
            flops=2 * TOK * DW * HV, bytes_accessed=9 * MIB, transcendentals=0
        ),
    )(order, cotangent, first, second, third)


def step_kernel(plan, params, moment, late, *refs):
    *terms, new_params, new_moment = refs
    gradient = add16(*[t[...] for t in terms]) * SCALE
    fresh = INNER_BETA * moment[...] + gradient
    new_moment[...] = fresh
    new_params[...] = params[...] - INNER_RATE * fresh
    rows = pl.ds(pl.multiple_of(plan[0] * FRAG, FRAG), FRAG)
    new_params[rows, :] = MIX_SHARE * new_params[rows, :] + MIX_SHARE * late[...]


def inner_step(plan, params, moment, late, terms):
    operands = [params, moment, late, *terms]
    return pl.pallas_call(
        step_kernel,
        out_shape=(jax.ShapeDtypeStruct((SLAB, HV), F32),) * 2,
        grid_spec=pltpu.PrefetchScalarGridSpec(
            num_scalar_prefetch=1,
            grid=(1,),
            in_specs=[whole(o.shape) for o in operands],
            out_specs=(whole((SLAB, HV)),) * 2,
        ),
        compiler_params=params_of(BIG),
        cost_estimate=pl.CostEstimate(flops=0, bytes_accessed=6 * MIB, transcendentals=0),
    )(plan, *operands)


def outer_kernel(plan, outer, moment, pending, new_outer, new_moment, late):
    rows = pl.ds(pl.multiple_of(plan[0] * FRAG, FRAG), FRAG)
    arrived = pending[...]
    new_outer[...] = outer[...]
    new_moment[...] = moment[...]
    moment_late = OUTER_BETA * moment[rows, :] + arrived
    outer_late = outer[rows, :] - OUTER_RATE * (arrived + OUTER_BETA * moment_late)
    new_moment[rows, :] = moment_late
    new_outer[rows, :] = outer_late
    late[...] = outer_late


def outer_step(plan, outer, moment, pending):
    operands = [outer, moment, pending]
    return pl.pallas_call(
        outer_kernel,
        out_shape=(
            jax.ShapeDtypeStruct((SLAB, HV), F32),
            jax.ShapeDtypeStruct((SLAB, HV), F32),
            jax.ShapeDtypeStruct((FRAG, HV), F32),
        ),
        grid_spec=pltpu.PrefetchScalarGridSpec(
            num_scalar_prefetch=1,
            grid=(1,),
            in_specs=[whole(o.shape) for o in operands],
            out_specs=(whole((SLAB, HV)), whole((SLAB, HV)), whole((FRAG, HV))),
        ),
        compiler_params=params_of(BIG),
        cost_estimate=pl.CostEstimate(flops=0, bytes_accessed=5 * MIB, transcendentals=0),
    )(plan, *operands)


def local_fragment(matrix, frag_index):
    return lax.dynamic_slice_in_dim(matrix, frag_index * FRAG, FRAG, 0)


def after(value, *others):
    return lax.optimization_barrier((value, *others))[0]


def body(activations, target, params, momentum, outer_params, outer_momentum, pending, plan):
    weights, moment = params[0], momentum[0]
    me, rep = lax.axis_index("fsdp"), lax.axis_index("rep")
    core = rep % 2
    relative = jnp.array(ORDER, jnp.int32)
    place = ((me // 4 + relative // 4) % 2) * 4 + (me % 4 + relative % 4) % 4

    w = weights.astype(BF16)
    w_back, w_next, w_z = move_y(w, 1), move_y(w, -1), move_z(w)

    turned = turn(place, after(activations, w))
    leaving = local_fragment(outer_params, plan[2]) - local_fragment(after(weights, w), plan[2])
    leaving = leaving.astype(BF16)
    half = FRAG // 2
    mine = lax.dynamic_slice_in_dim(leaving, core * half, half, 0)
    theirs = lax.dynamic_slice_in_dim(leaving, (1 - core) * half, half, 0)
    share = add_rounded(mine, swap_core(theirs))
    new_outer, new_outer_momentum, outer_late = outer_step(
        plan, after(outer_params, turned), outer_momentum, pending
    )

    a_z = w_z[:RA]
    az_back, az_next = move_y(a_z, 1), move_y(a_z, -1)
    far_lo, far_hi = move_y(w_back[:LO], 1), move_y(w_next[LO:], -1)
    bz_next, bz_back = move_z(w_next[RA:]), move_z(w_back[RA:])
    values, w_first = forward(place, FIRST, activations, [[w], [w_next], [w_back], [w_z]])
    share = add_rounded(share, swap_x(after(share, w_z), 1))
    share = add_rounded(share, swap_x(share, 3))

    az_lo, az_hi = move_y(az_back[:HA], 1), move_y(az_next[HA:], -1)
    bz_far = move_z(far_hi[RA - LO :])
    values, w_second = forward(
        place,
        SECOND,
        activations,
        [[far_lo, far_hi], [az_next, bz_next], [az_back, bz_back]],
        before=values,
    )
    cotangent, w_third = forward(
        place, THIRD, activations, [[az_lo, az_hi, bz_far]], before=values, target=target
    )

    z12_lo, z12_hi, z12_b, z11_a, z11_b, z13_a, z13_b, z02_lo, z02_hi = backward(
        turned, cotangent, 0, [[HA, HA, RB], [RA, RB], [RA, RB], [LO, SLAB - LO]]
    )
    z10, z01, z03, z00 = backward(turned, cotangent, 4, [[SLAB]] * 4)
    in11_lo, in13_hi = move_y(z12_lo, 1), move_y(z12_hi, -1)
    in02_b, in01_b, in03_b = move_z(z12_b), move_z(z11_b), move_z(z13_b)
    in01_lo = move_y(z02_lo, 1)

    grad_input = input_gradient(place, cotangent, w_first, w_second, w_third)

    to_next = jnp.concatenate([add_rounded(z11_a[:HA], in11_lo), z11_a[HA:]], 0)
    to_back = jnp.concatenate([z13_a[:HA], add_rounded(z13_a[HA:], in13_hi)], 0)
    in10_back, in10_next = move_y(to_next, 1), move_y(to_back, -1)
    in03_hi = move_y(jnp.concatenate([z02_hi[: RA - LO], add_rounded(z02_hi[RA - LO :], in02_b)], 0), -1)

    share = add_rounded(share, swap_z(after(share, in01_b), 1))
    share = add_rounded(share, swap_z(share, 3))

    z01, z03, z10 = after((z01, z03, z10), grad_input)
    to_next = jnp.concatenate(
        [add_rounded(z01[:LO], in01_lo), z01[LO:RA], add_rounded(z01[RA:], in01_b)], 0
    )
    to_back = jnp.concatenate(
        [
            z03[:LO],
            add_rounded(z03[LO:RA], in03_hi[: RA - LO]),
            add_rounded(z03[RA:], in03_hi[RA - LO :], in03_b),
        ],
        0,
    )
    in00_back, in00_next = move_y(to_next, 1), move_y(to_back, -1)
    across = jnp.concatenate([add_rounded(z10[:RA], in10_back, in10_next), z10[RA:]], 0)
    in00_z = move_z(across)

    other = swap_core(share)
    low, high = jnp.where(core == 0, share, other), jnp.where(core == 0, other, share)
    new_pending = jnp.concatenate([low, high], 0).astype(F32) / lax.axis_size("rep")

    new_params, new_moment = inner_step(
        plan, weights, moment, outer_late, [z00, in00_back, in00_next, in00_z]
    )
    return (
        new_params[None],
        new_moment[None],
        grad_input,
        new_outer,
        new_outer_momentum,
        new_pending,
    )


def solution(mesh):
    placed = (
        P(("rep", "fsdp"), None),
        P(("rep", "fsdp"), None),
        P("rep", "fsdp", None),
        P("rep", "fsdp", None),
        P("fsdp", None),
        P("fsdp", None),
        P("fsdp", None),
        P(),
    )
    return jax.shard_map(
        body,
        mesh=mesh,
        in_specs=placed,
        out_specs=(
            P("rep", "fsdp", None),
            P("rep", "fsdp", None),
            P(("rep", "fsdp"), None),
            P("fsdp", None),
            P("fsdp", None),
            P("fsdp", None),
        ),
        check_vma=False,
    )
```

```python
import functools

import jax
import jax.numpy as jnp
from jax import lax
from jax.experimental import pallas as pl
from jax.experimental.pallas import tpu as pltpu
from jax.sharding import PartitionSpec as P

DW = 4096
HV = 512
SLAB = 512
TOK = 512
NFRAG = 4
FRAG = SLAB // NFRAG
N_REP = 32
HALF = SLAB // 2
PART = HALF // 2
LOWER = 288
UPPER = SLAB - LOWER
SOME = LOWER // 2
ORDER = (6, 2, 3, 5, 7, 4, 1, 0)
AT = {shard: i for i, shard in enumerate(ORDER)}

INNER_RATE = 0.05
INNER_BETA = 0.9
OUTER_RATE = 0.7
OUTER_BETA = 0.9
MIX_SHARE = 0.5
SCALE = DW ** (-0.5)

F32 = jnp.float32
BF16 = jnp.bfloat16
MIB = 1024 * 1024
LIMIT = 16 * MIB
HINT = pl.CostEstimate(flops=1024, bytes_accessed=1024, transcendentals=0)


def move_y(value, step):
    pairs = [(z * 4 + y, z * 4 + (y + step) % 4) for z in range(2) for y in range(4)]
    return lax.ppermute(value, "fsdp", pairs)


def move_z(value):
    return lax.ppermute(value, "fsdp", [(i, (i + 4) % 8) for i in range(8)])


def swap_core(value):
    return lax.ppermute(value, "rep", [(i, i ^ 1) for i in range(32)])


def swap_x(value, flip):
    pairs = []
    for i in range(32):
        x = (i // 2) % 4
        pairs.append((i, i + 2 * ((x ^ flip) - x)))
    return lax.ppermute(value, "rep", pairs)


def swap_z(value, flip):
    pairs = []
    for i in range(32):
        h = i // 8
        pairs.append((i, i + 8 * ((h ^ flip) - h)))
    return lax.ppermute(value, "rep", pairs)


HBM = pl.BlockSpec(memory_space=pl.ANY)
SMEM = pl.BlockSpec(memory_space=pltpu.SMEM)
VMEM = pl.BlockSpec(memory_space=pltpu.VMEM)


def add16(*terms):
    total = terms[0].astype(F32)
    for term in terms[1:]:
        total = total + term.astype(F32)
    return total


def add_rounded(*terms):
    return add16(*terms).astype(BF16)


def start_all(pairs, sems, at=0):
    copies = []
    for i, (source, target) in enumerate(pairs):
        copy = pltpu.make_async_copy(source, target, sems.at[at + i])
        copy.start()
        copies.append(copy)
    return copies


def wait_all(copies):
    for copy in copies:
        copy.wait()


def local_call(kernel, near_outs, far_outs, scratch, scalars=(), near=(), far=(), late=(), aliases=None):
    outs = tuple(pltpu.VMEM(s, t) for s, t in near_outs)
    outs += tuple(pltpu.HBM(s, t) for s, t in far_outs)
    count = len(scalars) + len(near) + len(far)

    def run(*refs):
        kernel(*refs[:count], *refs[count + len(late) :])

    held = [pltpu.with_memory_space_constraint(a, pltpu.VMEM) for a in near]
    held += [pltpu.with_memory_space_constraint(a, pltpu.HBM) for a in far]
    held += [pltpu.with_memory_space_constraint(a, pltpu.HBM if in_hbm else pltpu.VMEM) for a, in_hbm in late]
    return pl.pallas_call(
        run,
        out_shape=outs,
        in_specs=[SMEM] * len(scalars) + [VMEM] * len(near) + [HBM] * (len(far) + len(late)),
        out_specs=(VMEM,) * len(near_outs) + (HBM,) * len(far_outs),
        scratch_shapes=scratch,
        input_output_aliases=aliases or {},
        compiler_params=pltpu.CompilerParams(vmem_limit_bytes=LIMIT),
        cost_estimate=HINT,
    )(*scalars, *held)


def rows16(rows):
    return ((rows, HV), BF16)


def slab_columns(where, shard):
    me = where[0]
    place = ((me // 4 + shard // 4) % 2) * 4 + (me % 4 + shard % 4) % 4
    return pl.ds(pl.multiple_of(place * SLAB, SLAB), SLAB)


def first_kernel(weights, w, w_lo, w_hi, held, sems):
    loads = [(weights.at[pl.ds(i * FRAG, FRAG)], held.at[pl.ds(i * FRAG, FRAG)]) for i in range(NFRAG)]
    for i, load in enumerate(start_all(loads, sems)):
        load.wait()
        part = held[i * FRAG : (i + 1) * FRAG].astype(BF16)
        w[i * FRAG : (i + 1) * FRAG] = part
        target, at = (w_lo, i * FRAG) if i < NFRAG // 2 else (w_hi, i * FRAG - HALF)
        target[at : at + FRAG] = part


def first(weights):
    scratch = [pltpu.VMEM((SLAB, HV), F32), pltpu.SemaphoreType.DMA((NFRAG,))]
    outs = [rows16(SLAB), rows16(HALF), rows16(HALF)]
    return local_call(first_kernel, outs, [], scratch, far=[weights])


def leaving_kernel(where, plan, weights, outer, mine, theirs, held, theta, sems):
    rows = pl.ds(pl.multiple_of(plan[2] * FRAG, FRAG), FRAG)
    wait_all(start_all([(weights.at[rows], held), (outer.at[rows], theta)], sems))
    theta[...] = theta[...] - held[...]
    half = FRAG // 2
    mine[...] = theta[pl.ds(pl.multiple_of(where[1] * half, half), half), :].astype(BF16)
    theirs[...] = theta[pl.ds(pl.multiple_of((1 - where[1]) * half, half), half), :].astype(BF16)


def leaving(where, plan, weights, outer, late):
    scratch = [pltpu.VMEM((FRAG, HV), F32), pltpu.VMEM((FRAG, HV), F32), pltpu.SemaphoreType.DMA((2,))]
    outs = [rows16(FRAG // 2)] * 2
    return local_call(leaving_kernel, outs, [], scratch, [where, plan], [], [weights, outer], late)


def turn_kernel(where, x, target, slabs, turned, goal, sems):
    loads = start_all([(x.at[:, slab_columns(where, d)], slabs.at[i]) for i, d in enumerate(ORDER)], sems)
    last = start_all([(target, goal)], sems, 8)
    for d in range(8):
        loads[d].wait()
        turned[d] = slabs[d].T
    wait_all(last)


def turn(where, activations, target, late):
    return local_call(
        turn_kernel,
        [((8, TOK, SLAB), BF16), ((8, SLAB, TOK), BF16), rows16(TOK)],
        [],
        [pltpu.SemaphoreType.DMA((9,))],
        [where],
        [],
        [activations, target],
        late,
    )


def share_kernel(mine, other, share):
    share[...] = add_rounded(mine[...], other[...])


def add_share(mine, other, late=()):
    return local_call(share_kernel, [rows16(FRAG // 2)], [], [], near=[mine, other], late=late)[0]


def share_first_kernel(held, mine, other, same, share):
    share[...] = add_rounded(mine[...], other[...])


def second_kernel(w_lo, w_hi, back_hi, next_hi, z_lo, mine, other, to_next, to_back, to_z, share):
    to_next[:HALF] = z_lo[...]
    to_next[HALF:] = back_hi[...]
    to_back[:HALF] = z_lo[...]
    to_back[HALF:] = w_lo[...]
    to_z[:HALF] = w_hi[...]
    to_z[HALF : 2 * HALF] = next_hi[...]
    to_z[2 * HALF :] = back_hi[...]
    share[...] = add_rounded(mine[...], other[...])


def third_kernel(w_lo, y_back, y_next, mine, other, to_next, to_back, to_z, share):
    to_next[:PART] = y_back[PART:HALF]
    to_next[PART:] = w_lo[...]
    to_back[:PART] = y_next[:PART]
    to_back[PART:] = y_next[HALF:]
    to_z[...] = y_back[HALF:]
    share[...] = add_rounded(mine[...], other[...])


def parts_of(parts, sources):
    values = [sources[source][at : at + rows] for source, at, rows in parts]
    return values[0] if len(values) == 1 else jnp.concatenate(values, axis=0)


def value_terms(table, slabs, sources):
    for shard, row, parts in table:
        weights = parts_of(parts, sources)
        columns = slabs[AT[shard], :, row : row + weights.shape[0]]
        yield jnp.dot(columns, weights, preferred_element_type=F32)


def forward_kernel(table, slabs, *refs):
    *sources, out = refs
    for j, term in enumerate(value_terms(table, slabs, sources)):
        out[...] = term if j == 0 else out[...] + term


def forward(slabs, sources, table, late):
    kernel = functools.partial(forward_kernel, table)
    return local_call(kernel, [((TOK, HV), F32)], [], [], near=[slabs, *sources], late=late)[0]


def middle_kernel(table, slabs, turned, before, target, y_back, y_next, z_far, *outs):
    cot, to_next, to_back, to_z, p02_hi, p03_hi = outs
    total = before[...]
    for term in value_terms(table, slabs, (y_back, y_next, z_far)):
        total = total + term
    cot[...] = (total * SCALE - target[...].astype(F32)).astype(BF16)
    p12, p02, p03 = (
        jnp.dot(turned[d], cot[...], preferred_element_type=F32).astype(BF16) for d in range(3)
    )
    to_next[:SOME] = p12[:SOME]
    to_next[SOME:] = p02[:LOWER]
    to_back[:SOME] = p12[SOME:LOWER]
    to_back[SOME:] = p03[:LOWER]
    to_z[...] = p12[LOWER:]
    p02_hi[...] = p02[LOWER:]
    p03_hi[...] = p03[LOWER:]


def middle(slabs, turned, before, target, sources, table):
    three = [rows16(SOME + LOWER), rows16(SOME + LOWER), rows16(UPPER)]
    return local_call(
        functools.partial(middle_kernel, table),
        [rows16(TOK)] + three + [rows16(UPPER)] * 2,
        [],
        [],
        near=[slabs, turned, before, target, *sources],
    )


def backward_kernel(turned, cot, p11_lo, p13_lo, p10_lo, to_z, p01, p00):
    for i, low in enumerate((p11_lo, p13_lo, p10_lo)):
        part = jnp.dot(turned[3 + i], cot[...], preferred_element_type=F32).astype(BF16)
        low[...] = part[:LOWER]
        to_z[i * UPPER : (i + 1) * UPPER] = part[LOWER:]
    p01[...] = jnp.dot(turned[6], cot[...], preferred_element_type=F32).astype(BF16)
    p00[...] = jnp.dot(turned[7], cot[...], preferred_element_type=F32).astype(BF16)


def input_kernel(table, where, cot, *refs):
    *sources, out, products, sems = refs
    stores = []
    for j, (shard, parts) in enumerate(table):
        product = lax.dot_general(
            cot[...],
            parts_of(parts, sources),
            (((1,), (1,)), ((), ())),
            preferred_element_type=F32,
        )
        products[j] = (product * SCALE).astype(BF16)
        stores += start_all([(products.at[j], out.at[:, slab_columns(where, shard)])], sems, j)
    wait_all(stores)


def input_gradient(where, cotangent, sources, table, late):
    by_shard = [(d, sum([p for s, _, p in sorted(table, key=lambda t: t[1]) if s == d], [])) for d in ORDER[::-1]]
    return local_call(
        functools.partial(input_kernel, by_shard),
        [],
        [((TOK, DW), BF16)],
        [pltpu.VMEM((8, TOK, SLAB), BF16), pltpu.SemaphoreType.DMA((8,))],
        [where],
        [cotangent, *sources],
        [],
        late,
    )[0]


def join_second_kernel(
    p11_lo, p13_lo, p01, p02_hi, from_back, from_next, in02_hi, to_next, to_back
):
    to_next[:SOME] = add_rounded(p11_lo[:SOME], from_back[:SOME])
    to_next[SOME:LOWER] = p11_lo[SOME:]
    to_next[LOWER:] = add_rounded(p01[:LOWER], from_back[SOME:])
    to_back[:SOME] = p13_lo[:SOME]
    to_back[SOME:LOWER] = add_rounded(p13_lo[SOME:], from_next[:SOME])
    to_back[LOWER:] = add_rounded(p02_hi[...], in02_hi[...])


def join_third_kernel(
    p01, p03_hi, p10_lo, from_back, from_next, in_hi, mine, other, to_next, to_back, to_z, share
):
    to_next[...] = add_rounded(p01[LOWER:], in_hi[:UPPER])
    to_back[...] = add_rounded(p03_hi[...], in_hi[UPPER : 2 * UPPER], from_next[LOWER:])
    to_z[...] = add_rounded(p10_lo[...], from_back[:LOWER], from_next[:LOWER])
    share[...] = add_rounded(mine[...], other[...])


def outer_kernel(plan, outer, moment, pending, params, inner, late, old, speed, new_outer, new_moment, held, push, came, sems):
    loads = start_all(
        [(outer, held), (moment, push), (pending, came), (params, old), (inner, speed)], sems
    )
    wait_all(loads[:3])
    rows = pl.ds(pl.multiple_of(plan[0] * FRAG, FRAG), FRAG)
    arrived = came[...]
    moment_late = OUTER_BETA * push[rows, :] + arrived
    outer_late = held[rows, :] - OUTER_RATE * (arrived + OUTER_BETA * moment_late)
    push[rows, :] = moment_late
    held[rows, :] = outer_late
    late[...] = outer_late
    stores = start_all([(held, new_outer), (push, new_moment)], sems, 5)
    wait_all(loads[3:] + stores)


def outer_step(plan, outer, moment, pending, params, inner, late):
    return local_call(
        outer_kernel,
        [((FRAG, HV), F32), ((SLAB, HV), F32), ((SLAB, HV), F32)],
        [((SLAB, HV), F32)] * 2,
        [
            pltpu.VMEM((SLAB, HV), F32),
            pltpu.VMEM((SLAB, HV), F32),
            pltpu.VMEM((FRAG, HV), F32),
            pltpu.SemaphoreType.DMA((7,)),
        ],
        [plan],
        [],
        [outer, moment, pending, params, inner],
        late,
    )


def step_kernel(where, plan, late, old, speed, share, other, own, low1, low2, low3, high1, high2, high3, *refs):
    new_params, new_moment, new_pending, params, moment, mean, sems = refs
    terms = [(low1, SOME), (low2, LOWER), (low3, 0)], [(high1, 2 * UPPER), (high2, 0), (high3, 0)]
    half = FRAG // 2
    mean[pl.ds(pl.multiple_of(where[1] * half, half), half), :] = share[...].astype(F32) / N_REP
    mean[pl.ds(pl.multiple_of((1 - where[1]) * half, half), half), :] = other[...].astype(F32) / N_REP
    stores = start_all([(mean, new_pending)], sems, 2 * NFRAG)
    for i in range(NFRAG):
        rows = pl.ds(i * FRAG, FRAG)
        first, end = i * FRAG, (i + 1) * FRAG
        cuts = [(0, first, min(end, LOWER)), (1, max(first, LOWER), end)]
        others = []
        for part, begin, stop in cuts:
            if begin < stop:
                at = begin - part * LOWER
                others.append(add16(*[t[row + at : row + at + stop - begin] for t, row in terms[part]]))
        others = others[0] if len(others) == 1 else jnp.concatenate(others, axis=0)
        fresh = INNER_BETA * speed[rows, :] + add16(own[rows, :], others) * SCALE
        moment[rows, :] = fresh
        stores += start_all([(moment.at[rows], new_moment.at[rows])], sems, 2 * i)
        stepped = old[rows, :] - INNER_RATE * fresh
        merged = MIX_SHARE * stepped + MIX_SHARE * late[...]
        params[rows, :] = jnp.where(plan[0] == i, merged, stepped)
        stores += start_all([(params.at[rows], new_params.at[rows])], sems, 2 * i + 1)
    wait_all(stores)


def inner_step(where, plan, near):
    return local_call(
        step_kernel,
        [],
        [((SLAB, HV), F32), ((SLAB, HV), F32), ((FRAG, HV), F32)],
        [
            pltpu.VMEM((SLAB, HV), F32),
            pltpu.VMEM((SLAB, HV), F32),
            pltpu.VMEM((FRAG, HV), F32),
            pltpu.SemaphoreType.DMA((2 * NFRAG + 1,)),
        ],
        [where, plan],
        near,
    )


def body(activations, target, params, momentum, outer_params, outer_momentum, pending, plan):
    weights, moment = params[0], momentum[0]
    where = jnp.stack([lax.axis_index("fsdp"), lax.axis_index("rep") % 2]).astype(jnp.int32)
    share_rows = rows16(FRAG // 2)

    w, w_lo, w_hi = first(weights)
    z_lo, back_hi, next_hi = move_z(w_lo), move_y(w_hi, 1), move_y(w_hi, -1)
    mine, theirs = leaving(where, plan, weights, outer_params, [(w, False)])
    other = swap_core(theirs)

    to_next, to_back, to_z, share = local_call(
        second_kernel,
        [rows16(2 * HALF), rows16(2 * HALF), rows16(3 * HALF), share_rows],
        [],
        [],
        near=[w_lo, w_hi, back_hi, next_hi, z_lo, mine, other],
    )
    z_hi, y_back, y_next = move_z(to_z), move_y(to_next, 1), move_y(to_back, -1)
    slabs, turned, goal = turn(where, activations, target, [(share, False)])
    share = add_share(share, swap_x(share, 1))
    other = swap_x(share, 3)

    to_next, to_back, to_z, share = local_call(
        third_kernel,
        [rows16(PART + HALF), rows16(PART + HALF), rows16(HALF), share_rows],
        [],
        [],
        near=[w_lo, y_back, y_next, share, other],
        late=[(goal, False)],
    )
    z_far, y_back3, y_next3 = move_z(to_z), move_y(to_next, 1), move_y(to_back, -1)
    other = swap_z(share, 1)

    near = [w, next_hi, back_hi, z_lo, y_back, y_next, z_hi]
    upper = SLAB - HALF
    table = [
        (0, 0, [(0, 0, SLAB)]),
        (1, 0, [(5, HALF, HALF), (1, 0, upper)]),
        (4, 0, [(3, 0, HALF), (6, 0, upper)]),
        (5, 0, [(5, 0, HALF), (6, HALF, upper)]),
        (7, 0, [(4, 0, HALF), (6, 2 * HALF, upper)]),
        (3, HALF, [(2, 0, upper)]),
        (2, HALF, [(4, HALF, upper)]),
    ]
    late, old, speed, new_outer, new_outer_momentum = outer_step(
        plan, outer_params, outer_momentum, pending, weights, moment, [(to_z, False)]
    )
    values = forward(slabs, near, table, [(late, False)])
    last = [y_back3, y_next3, z_far]
    cotangent, to_next, to_back, to_z, p02_hi, p03_hi = middle(
        slabs,
        turned,
        values,
        goal,
        last,
        [
            (3, 0, [(0, PART, HALF)]),
            (2, 0, [(1, PART, HALF)]),
            (6, 0, [(1, 0, PART), (0, 0, PART), (2, 0, upper)]),
        ],
    )

    in02_hi, from_back, from_next = move_z(to_z), move_y(to_next, 1), move_y(to_back, -1)
    low1 = from_next
    p11_lo, p13_lo, p10_lo, to_z, p01, p00 = local_call(
        backward_kernel,
        [rows16(LOWER)] * 3 + [rows16(3 * UPPER), rows16(SLAB), rows16(SLAB)],
        [],
        [],
        near=[turned, cotangent],
    )
    to_z, share = local_call(
        share_first_kernel,
        [rows16(3 * UPPER), share_rows],
        [],
        [],
        near=[to_z, share, other],
        aliases={0: 0},
    )
    in_hi = move_z(to_z)

    to_next, to_back = local_call(
        join_second_kernel,
        [rows16(2 * LOWER), rows16(SLAB)],
        [],
        [],
        near=[p11_lo, p13_lo, p01, p02_hi, from_back, from_next, in02_hi],
    )
    from_back, from_next = move_y(to_next, 1), move_y(to_back, -1)
    low2 = from_back
    other = swap_z(share, 3)
    table += [
        (3, 0, [(7, PART, HALF)]),
        (2, 0, [(8, PART, HALF)]),
        (6, 0, [(8, 0, PART), (7, 0, PART), (9, 0, upper)]),
    ]
    grad_input = input_gradient(where, cotangent, near + last, table, [(to_back, False)])

    to_next, to_back, to_z, share = local_call(
        join_third_kernel,
        [rows16(UPPER), rows16(UPPER), rows16(LOWER), share_rows],
        [],
        [],
        near=[p01, p03_hi, p10_lo, from_back, from_next, in_hi, share, other],
        late=[(grad_input, True)],
    )
    low3, high2, high3 = move_z(to_z), move_y(to_next, 1), move_y(to_back, -1)
    other = swap_core(share)

    terms = [p00, low1, low2, low3, in_hi, high2, high3]
    new_params, new_moment, new_pending = inner_step(
        where, plan, [late, old, speed, share, other, *terms]
    )
    return (
        new_params[None],
        new_moment[None],
        grad_input,
        new_outer,
        new_outer_momentum,
        new_pending,
    )


def solution(mesh):
    placed = (
        P(("rep", "fsdp"), None),
        P(("rep", "fsdp"), None),
        P("rep", "fsdp", None),
        P("rep", "fsdp", None),
        P("fsdp", None),
        P("fsdp", None),
        P("fsdp", None),
        P(),
    )
    return jax.shard_map(
        body,
        mesh=mesh,
        in_specs=placed,
        out_specs=(
            P("rep", "fsdp", None),
            P("rep", "fsdp", None),
            P(("rep", "fsdp"), None),
            P("fsdp", None),
            P("fsdp", None),
            P("fsdp", None),
        ),
        check_vma=False,
    )
```

```python
import functools

import jax
import jax.numpy as jnp
from jax import lax
from jax.experimental import pallas as pl
from jax.experimental.pallas import tpu as pltpu
from jax.sharding import PartitionSpec as P

DW = 4096
HV = 512
SLAB = 512
TOK = 512
NFRAG = 4
FRAG = SLAB // NFRAG
N_REP = 32
HALF = SLAB // 2
PART = HALF // 2
LOWER = 288
UPPER = SLAB - LOWER
SOME = LOWER // 2
ORDER = (6, 2, 3, 5, 7, 4, 1, 0)
AT = {shard: i for i, shard in enumerate(ORDER)}

INNER_RATE = 0.05
INNER_BETA = 0.9
OUTER_RATE = 0.7
OUTER_BETA = 0.9
MIX_SHARE = 0.5
SCALE = DW ** (-0.5)

F32 = jnp.float32
BF16 = jnp.bfloat16
MIB = 1024 * 1024
LIMIT = 16 * MIB
HINT = pl.CostEstimate(flops=1024, bytes_accessed=1024, transcendentals=0)


def move_y(value, step):
    pairs = [(z * 4 + y, z * 4 + (y + step) % 4) for z in range(2) for y in range(4)]
    return lax.ppermute(value, "fsdp", pairs)


def move_z(value):
    return lax.ppermute(value, "fsdp", [(i, (i + 4) % 8) for i in range(8)])


def swap_core(value):
    return lax.ppermute(value, "rep", [(i, i ^ 1) for i in range(32)])


def swap_x(value, flip):
    pairs = []
    for i in range(32):
        x = (i // 2) % 4
        pairs.append((i, i + 2 * ((x ^ flip) - x)))
    return lax.ppermute(value, "rep", pairs)


def swap_z(value, flip):
    pairs = []
    for i in range(32):
        h = i // 8
        pairs.append((i, i + 8 * ((h ^ flip) - h)))
    return lax.ppermute(value, "rep", pairs)


HBM = pl.BlockSpec(memory_space=pl.ANY)
SMEM = pl.BlockSpec(memory_space=pltpu.SMEM)
VMEM = pl.BlockSpec(memory_space=pltpu.VMEM)


def add16(*terms):
    total = terms[0].astype(F32)
    for term in terms[1:]:
        total = total + term.astype(F32)
    return total


def add_rounded(*terms):
    return add16(*terms).astype(BF16)


def start_all(pairs, sems, at=0):
    copies = []
    for i, (source, target) in enumerate(pairs):
        copy = pltpu.make_async_copy(source, target, sems.at[at + i])
        copy.start()
        copies.append(copy)
    return copies


def wait_all(copies):
    for copy in copies:
        copy.wait()


def local_call(kernel, near_outs, far_outs, scratch, scalars=(), near=(), far=(), late=(), aliases=None):
    outs = tuple(pltpu.VMEM(s, t) for s, t in near_outs)
    outs += tuple(pltpu.HBM(s, t) for s, t in far_outs)
    count = len(scalars) + len(near) + len(far)

    def run(*refs):
        kernel(*refs[:count], *refs[count + len(late) :])

    held = [pltpu.with_memory_space_constraint(a, pltpu.VMEM) for a in near]
    held += [pltpu.with_memory_space_constraint(a, pltpu.HBM) for a in far]
    held += [pltpu.with_memory_space_constraint(a, pltpu.HBM if in_hbm else pltpu.VMEM) for a, in_hbm in late]
    return pl.pallas_call(
        run,
        out_shape=outs,
        in_specs=[SMEM] * len(scalars) + [VMEM] * len(near) + [HBM] * (len(far) + len(late)),
        out_specs=(VMEM,) * len(near_outs) + (HBM,) * len(far_outs),
        scratch_shapes=scratch,
        input_output_aliases=aliases or {},
        compiler_params=pltpu.CompilerParams(vmem_limit_bytes=LIMIT),
        cost_estimate=HINT,
    )(*scalars, *held)


def rows16(rows):
    return ((rows, HV), BF16)


def slab_columns(where, shard):
    me = where[0]
    place = ((me // 4 + shard // 4) % 2) * 4 + (me % 4 + shard % 4) % 4
    return pl.ds(pl.multiple_of(place * SLAB, SLAB), SLAB)


def first_kernel(weights, w, w_lo, w_hi, held, sems):
    loads = [(weights.at[pl.ds(i * FRAG, FRAG)], held.at[pl.ds(i * FRAG, FRAG)]) for i in range(NFRAG)]
    for i, load in enumerate(start_all(loads, sems)):
        load.wait()
        part = held[i * FRAG : (i + 1) * FRAG].astype(BF16)
        w[i * FRAG : (i + 1) * FRAG] = part
        target, at = (w_lo, i * FRAG) if i < NFRAG // 2 else (w_hi, i * FRAG - HALF)
        target[at : at + FRAG] = part


def first(weights):
    scratch = [pltpu.VMEM((SLAB, HV), F32), pltpu.SemaphoreType.DMA((NFRAG,))]
    outs = [rows16(SLAB), rows16(HALF), rows16(HALF)]
    return local_call(first_kernel, outs, [], scratch, far=[weights])


def leaving_kernel(where, plan, weights, outer, mine, theirs, held, theta, sems):
    rows = pl.ds(pl.multiple_of(plan[2] * FRAG, FRAG), FRAG)
    wait_all(start_all([(weights.at[rows], held), (outer.at[rows], theta)], sems))
    theta[...] = theta[...] - held[...]
    half = FRAG // 2
    mine[...] = theta[pl.ds(pl.multiple_of(where[1] * half, half), half), :].astype(BF16)
    theirs[...] = theta[pl.ds(pl.multiple_of((1 - where[1]) * half, half), half), :].astype(BF16)


def leaving(where, plan, weights, outer, late):
    scratch = [pltpu.VMEM((FRAG, HV), F32), pltpu.VMEM((FRAG, HV), F32), pltpu.SemaphoreType.DMA((2,))]
    outs = [rows16(FRAG // 2)] * 2
    return local_call(leaving_kernel, outs, [], scratch, [where, plan], [], [weights, outer], late)


def turn_kernel(where, x, target, slabs, turned, goal, sems):
    loads = start_all([(x.at[:, slab_columns(where, d)], slabs.at[i]) for i, d in enumerate(ORDER)], sems)
    last = start_all([(target, goal)], sems, 8)
    for d in range(8):
        loads[d].wait()
        turned[d] = slabs[d].T
    wait_all(last)


def turn(where, activations, target, late):
    return local_call(
        turn_kernel,
        [((8, TOK, SLAB), BF16), ((8, SLAB, TOK), BF16), rows16(TOK)],
        [],
        [pltpu.SemaphoreType.DMA((9,))],
        [where],
        [],
        [activations, target],
        late,
    )


def share_kernel(mine, other, share):
    share[...] = add_rounded(mine[...], other[...])


def add_share(mine, other, late=()):
    return local_call(share_kernel, [rows16(FRAG // 2)], [], [], near=[mine, other], late=late)[0]


def share_first_kernel(held, mine, other, same, share):
    share[...] = add_rounded(mine[...], other[...])


def second_y_kernel(w_lo, back_hi, z_lo, mine, other, to_next, to_back, share):
    to_next[:HALF] = z_lo[...]
    to_next[HALF:] = back_hi[...]
    to_back[:HALF] = z_lo[...]
    to_back[HALF:] = w_lo[...]
    share[...] = add_rounded(mine[...], other[...])


def second_z_kernel(w_hi, back_hi, next_hi, to_z):
    to_z[:HALF] = w_hi[...]
    to_z[HALF : 2 * HALF] = next_hi[...]
    to_z[2 * HALF :] = back_hi[...]


def third_kernel(w_lo, y_back, y_next, mine, other, to_next, to_back, to_z, share):
    to_next[:PART] = y_back[PART:HALF]
    to_next[PART:] = w_lo[...]
    to_back[:PART] = y_next[:PART]
    to_back[PART:] = y_next[HALF:]
    to_z[...] = y_back[HALF:]
    share[...] = add_rounded(mine[...], other[...])


def parts_of(parts, sources):
    values = [sources[source][at : at + rows] for source, at, rows in parts]
    return values[0] if len(values) == 1 else jnp.concatenate(values, axis=0)


def value_terms(table, slabs, sources):
    for shard, row, parts in table:
        weights = parts_of(parts, sources)
        columns = slabs[AT[shard], :, row : row + weights.shape[0]]
        yield jnp.dot(columns, weights, preferred_element_type=F32)


def forward_kernel(table, slabs, *refs):
    *sources, out = refs
    for j, term in enumerate(value_terms(table, slabs, sources)):
        out[...] = term if j == 0 else out[...] + term


def forward(slabs, sources, table, late):
    kernel = functools.partial(forward_kernel, table)
    return local_call(kernel, [((TOK, HV), F32)], [], [], near=[slabs, *sources], late=late)[0]


def middle_kernel(table, slabs, turned, before, target, y_back, y_next, z_far, *outs):
    cot, to_next, to_back, to_z, p02_hi, p03_hi = outs
    total = before[...]
    for term in value_terms(table, slabs, (y_back, y_next, z_far)):
        total = total + term
    cot[...] = (total * SCALE - target[...].astype(F32)).astype(BF16)
    p12, p02, p03 = (
        jnp.dot(turned[d], cot[...], preferred_element_type=F32).astype(BF16) for d in range(3)
    )
    to_next[:SOME] = p12[:SOME]
    to_next[SOME:] = p02[:LOWER]
    to_back[:SOME] = p12[SOME:LOWER]
    to_back[SOME:] = p03[:LOWER]
    to_z[...] = p12[LOWER:]
    p02_hi[...] = p02[LOWER:]
    p03_hi[...] = p03[LOWER:]


def middle(slabs, turned, before, target, sources, table):
    three = [rows16(SOME + LOWER), rows16(SOME + LOWER), rows16(UPPER)]
    return local_call(
        functools.partial(middle_kernel, table),
        [rows16(TOK)] + three + [rows16(UPPER)] * 2,
        [],
        [],
        near=[slabs, turned, before, target, *sources],
    )


def backward_kernel(turned, cot, p11_lo, p13_lo, p10_lo, to_z, p01, p00):
    for i, low in enumerate((p11_lo, p13_lo, p10_lo)):
        part = jnp.dot(turned[3 + i], cot[...], preferred_element_type=F32).astype(BF16)
        low[...] = part[:LOWER]
        to_z[i * UPPER : (i + 1) * UPPER] = part[LOWER:]
    p01[...] = jnp.dot(turned[6], cot[...], preferred_element_type=F32).astype(BF16)
    p00[...] = jnp.dot(turned[7], cot[...], preferred_element_type=F32).astype(BF16)


def input_kernel(table, where, cot, *refs):
    *sources, out, products, sems = refs
    stores = []
    for j, (shard, parts) in enumerate(table):
        product = lax.dot_general(
            cot[...],
            parts_of(parts, sources),
            (((1,), (1,)), ((), ())),
            preferred_element_type=F32,
        )
        products[j] = (product * SCALE).astype(BF16)
        stores += start_all([(products.at[j], out.at[:, slab_columns(where, shard)])], sems, j)
    wait_all(stores)


def input_gradient(where, cotangent, sources, table, late):
    by_shard = [(d, sum([p for s, _, p in sorted(table, key=lambda t: t[1]) if s == d], [])) for d in ORDER[::-1]]
    return local_call(
        functools.partial(input_kernel, by_shard),
        [],
        [((TOK, DW), BF16)],
        [pltpu.VMEM((8, TOK, SLAB), BF16), pltpu.SemaphoreType.DMA((8,))],
        [where],
        [cotangent, *sources],
        [],
        late,
    )[0]


def join_second_a_kernel(p11_lo, p01, from_back, to_next):
    to_next[:SOME] = add_rounded(p11_lo[:SOME], from_back[:SOME])
    to_next[SOME:LOWER] = p11_lo[SOME:]
    to_next[LOWER:] = add_rounded(p01[:LOWER], from_back[SOME:])


def join_second_b_kernel(p13_lo, p02_hi, from_next, in02_hi, to_back):
    to_back[:SOME] = p13_lo[:SOME]
    to_back[SOME:LOWER] = add_rounded(p13_lo[SOME:], from_next[:SOME])
    to_back[LOWER:] = add_rounded(p02_hi[...], in02_hi[...])


def join_third_kernel(
    p01, p03_hi, p10_lo, from_back, from_next, in_hi, mine, other, to_next, to_back, to_z, share
):
    to_next[...] = add_rounded(p01[LOWER:], in_hi[:UPPER])
    to_back[...] = add_rounded(p03_hi[...], in_hi[UPPER : 2 * UPPER], from_next[LOWER:])
    to_z[...] = add_rounded(p10_lo[...], from_back[:LOWER], from_next[:LOWER])
    share[...] = add_rounded(mine[...], other[...])


def outer_kernel(plan, outer, moment, pending, params, inner, late, old, speed, new_outer, new_moment, held, push, came, sems):
    loads = start_all(
        [(outer, held), (moment, push), (pending, came), (params, old), (inner, speed)], sems
    )
    wait_all(loads[:3])
    rows = pl.ds(pl.multiple_of(plan[0] * FRAG, FRAG), FRAG)
    arrived = came[...]
    moment_late = OUTER_BETA * push[rows, :] + arrived
    outer_late = held[rows, :] - OUTER_RATE * (arrived + OUTER_BETA * moment_late)
    push[rows, :] = moment_late
    held[rows, :] = outer_late
    late[...] = outer_late
    stores = start_all([(held, new_outer), (push, new_moment)], sems, 5)
    wait_all(loads[3:] + stores)


def outer_step(plan, outer, moment, pending, params, inner, late):
    return local_call(
        outer_kernel,
        [((FRAG, HV), F32), ((SLAB, HV), F32), ((SLAB, HV), F32)],
        [((SLAB, HV), F32)] * 2,
        [
            pltpu.VMEM((SLAB, HV), F32),
            pltpu.VMEM((SLAB, HV), F32),
            pltpu.VMEM((FRAG, HV), F32),
            pltpu.SemaphoreType.DMA((7,)),
        ],
        [plan],
        [],
        [outer, moment, pending, params, inner],
        late,
    )


def step_kernel(where, plan, late, old, speed, share, other, own, low1, low2, low3, high1, high2, high3, *refs):
    new_params, new_moment, new_pending, params, moment, mean, sems = refs
    terms = [(low1, SOME), (low2, LOWER), (low3, 0)], [(high1, 2 * UPPER), (high2, 0), (high3, 0)]
    half = FRAG // 2
    mean[pl.ds(pl.multiple_of(where[1] * half, half), half), :] = share[...].astype(F32) / N_REP
    mean[pl.ds(pl.multiple_of((1 - where[1]) * half, half), half), :] = other[...].astype(F32) / N_REP
    stores = start_all([(mean, new_pending)], sems, 2 * NFRAG)
    for i in range(NFRAG):
        rows = pl.ds(i * FRAG, FRAG)
        first, end = i * FRAG, (i + 1) * FRAG
        cuts = [(0, first, min(end, LOWER)), (1, max(first, LOWER), end)]
        others = []
        for part, begin, stop in cuts:
            if begin < stop:
                at = begin - part * LOWER
                others.append(add16(*[t[row + at : row + at + stop - begin] for t, row in terms[part]]))
        others = others[0] if len(others) == 1 else jnp.concatenate(others, axis=0)
        fresh = INNER_BETA * speed[rows, :] + add16(own[rows, :], others) * SCALE
        moment[rows, :] = fresh
        stores += start_all([(moment.at[rows], new_moment.at[rows])], sems, 2 * i)
        stepped = old[rows, :] - INNER_RATE * fresh
        merged = MIX_SHARE * stepped + MIX_SHARE * late[...]
        params[rows, :] = jnp.where(plan[0] == i, merged, stepped)
        stores += start_all([(params.at[rows], new_params.at[rows])], sems, 2 * i + 1)
    wait_all(stores)


def inner_step(where, plan, near):
    return local_call(
        step_kernel,
        [],
        [((SLAB, HV), F32), ((SLAB, HV), F32), ((FRAG, HV), F32)],
        [
            pltpu.VMEM((SLAB, HV), F32),
            pltpu.VMEM((SLAB, HV), F32),
            pltpu.VMEM((FRAG, HV), F32),
            pltpu.SemaphoreType.DMA((2 * NFRAG + 1,)),
        ],
        [where, plan],
        near,
    )


def body(activations, target, params, momentum, outer_params, outer_momentum, pending, plan):
    weights, moment = params[0], momentum[0]
    where = jnp.stack([lax.axis_index("fsdp"), lax.axis_index("rep") % 2]).astype(jnp.int32)
    share_rows = rows16(FRAG // 2)

    w, w_lo, w_hi = first(weights)
    z_lo, back_hi, next_hi = move_z(w_lo), move_y(w_hi, 1), move_y(w_hi, -1)
    mine, theirs = leaving(where, plan, weights, outer_params, [(w, False)])
    other = swap_core(theirs)

    to_next, to_back, share = local_call(
        second_y_kernel,
        [rows16(2 * HALF), rows16(2 * HALF), share_rows],
        [],
        [],
        near=[w_lo, back_hi, z_lo, mine, other],
    )
    to_z = local_call(
        second_z_kernel, [rows16(3 * HALF)], [], [], near=[w_hi, back_hi, next_hi]
    )[0]
    z_hi, y_back, y_next = move_z(to_z), move_y(to_next, 1), move_y(to_back, -1)
    slabs, turned, goal = turn(where, activations, target, [(share, False)])
    share = add_share(share, swap_x(share, 1))
    other = swap_x(share, 3)

    to_next, to_back, to_z, share = local_call(
        third_kernel,
        [rows16(PART + HALF), rows16(PART + HALF), rows16(HALF), share_rows],
        [],
        [],
        near=[w_lo, y_back, y_next, share, other],
        late=[(goal, False)],
    )
    z_far, y_back3, y_next3 = move_z(to_z), move_y(to_next, 1), move_y(to_back, -1)
    other = swap_z(share, 1)

    near = [w, next_hi, back_hi, z_lo, y_back, y_next, z_hi]
    upper = SLAB - HALF
    table = [
        (0, 0, [(0, 0, SLAB)]),
        (1, 0, [(5, HALF, HALF), (1, 0, upper)]),
        (4, 0, [(3, 0, HALF), (6, 0, upper)]),
        (5, 0, [(5, 0, HALF), (6, HALF, upper)]),
        (7, 0, [(4, 0, HALF), (6, 2 * HALF, upper)]),
        (3, HALF, [(2, 0, upper)]),
        (2, HALF, [(4, HALF, upper)]),
    ]
    late, old, speed, new_outer, new_outer_momentum = outer_step(
        plan, outer_params, outer_momentum, pending, weights, moment, [(to_z, False)]
    )
    values = forward(slabs, near, table, [(late, False)])
    last = [y_back3, y_next3, z_far]
    cotangent, to_next, to_back, to_z, p02_hi, p03_hi = middle(
        slabs,
        turned,
        values,
        goal,
        last,
        [
            (3, 0, [(0, PART, HALF)]),
            (2, 0, [(1, PART, HALF)]),
            (6, 0, [(1, 0, PART), (0, 0, PART), (2, 0, upper)]),
        ],
    )

    in02_hi, from_back, from_next = move_z(to_z), move_y(to_next, 1), move_y(to_back, -1)
    low1 = from_next
    p11_lo, p13_lo, p10_lo, to_z, p01, p00 = local_call(
        backward_kernel,
        [rows16(LOWER)] * 3 + [rows16(3 * UPPER), rows16(SLAB), rows16(SLAB)],
        [],
        [],
        near=[turned, cotangent],
    )
    to_z, share = local_call(
        share_first_kernel,
        [rows16(3 * UPPER), share_rows],
        [],
        [],
        near=[to_z, share, other],
        aliases={0: 0},
    )
    in_hi = move_z(to_z)

    to_next = local_call(
        join_second_a_kernel, [rows16(2 * LOWER)], [], [], near=[p11_lo, p01, from_back]
    )[0]
    to_back = local_call(
        join_second_b_kernel,
        [rows16(SLAB)],
        [],
        [],
        near=[p13_lo, p02_hi, from_next, in02_hi],
        late=[(to_next, False)],
    )[0]
    from_back, from_next = move_y(to_next, 1), move_y(to_back, -1)
    low2 = from_back
    other = swap_z(share, 3)
    table += [
        (3, 0, [(7, PART, HALF)]),
        (2, 0, [(8, PART, HALF)]),
        (6, 0, [(8, 0, PART), (7, 0, PART), (9, 0, upper)]),
    ]
    grad_input = input_gradient(where, cotangent, near + last, table, [(to_back, False)])

    to_next, to_back, to_z, share = local_call(
        join_third_kernel,
        [rows16(UPPER), rows16(UPPER), rows16(LOWER), share_rows],
        [],
        [],
        near=[p01, p03_hi, p10_lo, from_back, from_next, in_hi, share, other],
        late=[(grad_input, True)],
    )
    low3, high2, high3 = move_z(to_z), move_y(to_next, 1), move_y(to_back, -1)
    other = swap_core(share)

    terms = [p00, low1, low2, low3, in_hi, high2, high3]
    new_params, new_moment, new_pending = inner_step(
        where, plan, [late, old, speed, share, other, *terms]
    )
    return (
        new_params[None],
        new_moment[None],
        grad_input,
        new_outer,
        new_outer_momentum,
        new_pending,
    )


def solution(mesh):
    placed = (
        P(("rep", "fsdp"), None),
        P(("rep", "fsdp"), None),
        P("rep", "fsdp", None),
        P("rep", "fsdp", None),
        P("fsdp", None),
        P("fsdp", None),
        P("fsdp", None),
        P(),
    )
    return jax.shard_map(
        body,
        mesh=mesh,
        in_specs=placed,
        out_specs=(
            P("rep", "fsdp", None),
            P("rep", "fsdp", None),
            P(("rep", "fsdp"), None),
            P("fsdp", None),
            P("fsdp", None),
            P("fsdp", None),
        ),
        check_vma=False,
    )
```

```python
import functools

import jax
import jax.numpy as jnp
from jax import lax
from jax.experimental import pallas as pl
from jax.experimental.pallas import tpu as pltpu
from jax.sharding import PartitionSpec as P

DW = 4096
HV = 512
SLAB = 512
TOK = 512
NFRAG = 4
FRAG = SLAB // NFRAG
N_REP = 32
HALF = SLAB // 2
PART = HALF // 2
LOWER = 320
UPPER = SLAB - LOWER
SOME = LOWER // 2
ORDER = (6, 2, 3, 5, 7, 4, 1, 0)
AT = {shard: i for i, shard in enumerate(ORDER)}

INNER_RATE = 0.05
INNER_BETA = 0.9
OUTER_RATE = 0.7
OUTER_BETA = 0.9
MIX_SHARE = 0.5
SCALE = DW ** (-0.5)

F32 = jnp.float32
BF16 = jnp.bfloat16
MIB = 1024 * 1024
LIMIT = 16 * MIB
HINT = pl.CostEstimate(flops=1024, bytes_accessed=1024, transcendentals=0)


def move_y(value, step):
    pairs = [(z * 4 + y, z * 4 + (y + step) % 4) for z in range(2) for y in range(4)]
    return lax.ppermute(value, "fsdp", pairs)


def move_z(value):
    return lax.ppermute(value, "fsdp", [(i, (i + 4) % 8) for i in range(8)])


def swap_core(value):
    return lax.ppermute(value, "rep", [(i, i ^ 1) for i in range(32)])


def swap_x(value, flip):
    pairs = []
    for i in range(32):
        x = (i // 2) % 4
        pairs.append((i, i + 2 * ((x ^ flip) - x)))
    return lax.ppermute(value, "rep", pairs)


def swap_z(value, flip):
    pairs = []
    for i in range(32):
        h = i // 8
        pairs.append((i, i + 8 * ((h ^ flip) - h)))
    return lax.ppermute(value, "rep", pairs)


HBM = pl.BlockSpec(memory_space=pl.ANY)
SMEM = pl.BlockSpec(memory_space=pltpu.SMEM)
VMEM = pl.BlockSpec(memory_space=pltpu.VMEM)


def add16(*terms):
    total = terms[0].astype(F32)
    for term in terms[1:]:
        total = total + term.astype(F32)
    return total


def add_rounded(*terms):
    return add16(*terms).astype(BF16)


def start_all(pairs, sems, at=0):
    copies = []
    for i, (source, target) in enumerate(pairs):
        copy = pltpu.make_async_copy(source, target, sems.at[at + i])
        copy.start()
        copies.append(copy)
    return copies


def wait_all(copies):
    for copy in copies:
        copy.wait()


def local_call(kernel, near_outs, far_outs, scratch, scalars=(), near=(), far=(), late=(), aliases=None):
    outs = tuple(pltpu.VMEM(s, t) for s, t in near_outs)
    outs += tuple(pltpu.HBM(s, t) for s, t in far_outs)
    count = len(scalars) + len(near) + len(far)

    def run(*refs):
        kernel(*refs[:count], *refs[count + len(late) :])

    held = [pltpu.with_memory_space_constraint(a, pltpu.VMEM) for a in near]
    held += [pltpu.with_memory_space_constraint(a, pltpu.HBM) for a in far]
    held += [pltpu.with_memory_space_constraint(a, pltpu.HBM if in_hbm else pltpu.VMEM) for a, in_hbm in late]
    return pl.pallas_call(
        run,
        out_shape=outs,
        in_specs=[SMEM] * len(scalars) + [VMEM] * len(near) + [HBM] * (len(far) + len(late)),
        out_specs=(VMEM,) * len(near_outs) + (HBM,) * len(far_outs),
        scratch_shapes=scratch,
        input_output_aliases=aliases or {},
        compiler_params=pltpu.CompilerParams(vmem_limit_bytes=LIMIT),
        cost_estimate=HINT,
    )(*scalars, *held)


def rows16(rows):
    return ((rows, HV), BF16)


def slab_columns(where, shard):
    me = where[0]
    place = ((me // 4 + shard // 4) % 2) * 4 + (me % 4 + shard % 4) % 4
    return pl.ds(pl.multiple_of(place * SLAB, SLAB), SLAB)


def first_kernel(weights, w, w_lo, w_hi, held, sems):
    loads = [(weights.at[pl.ds(i * FRAG, FRAG)], held.at[pl.ds(i * FRAG, FRAG)]) for i in range(NFRAG)]
    for i, load in enumerate(start_all(loads, sems)):
        load.wait()
        part = held[i * FRAG : (i + 1) * FRAG].astype(BF16)
        w[i * FRAG : (i + 1) * FRAG] = part
        target, at = (w_lo, i * FRAG) if i < NFRAG // 2 else (w_hi, i * FRAG - HALF)
        target[at : at + FRAG] = part


def first(weights):
    scratch = [pltpu.VMEM((SLAB, HV), F32), pltpu.SemaphoreType.DMA((NFRAG,))]
    outs = [rows16(SLAB), rows16(HALF), rows16(HALF)]
    return local_call(first_kernel, outs, [], scratch, far=[weights])


def leaving_kernel(where, plan, weights, outer, mine, theirs, held, theta, sems):
    rows = pl.ds(pl.multiple_of(plan[2] * FRAG, FRAG), FRAG)
    wait_all(start_all([(weights.at[rows], held), (outer.at[rows], theta)], sems))
    theta[...] = theta[...] - held[...]
    half = FRAG // 2
    mine[...] = theta[pl.ds(pl.multiple_of(where[1] * half, half), half), :].astype(BF16)
    theirs[...] = theta[pl.ds(pl.multiple_of((1 - where[1]) * half, half), half), :].astype(BF16)


def leaving(where, plan, weights, outer, late):
    scratch = [pltpu.VMEM((FRAG, HV), F32), pltpu.VMEM((FRAG, HV), F32), pltpu.SemaphoreType.DMA((2,))]
    outs = [rows16(FRAG // 2)] * 2
    return local_call(leaving_kernel, outs, [], scratch, [where, plan], [], [weights, outer], late)


def turn_kernel(where, x, target, slabs, turned, goal, sems):
    loads = start_all([(x.at[:, slab_columns(where, d)], slabs.at[i]) for i, d in enumerate(ORDER)], sems)
    last = start_all([(target, goal)], sems, 8)
    for d in range(8):
        loads[d].wait()
        turned[d] = slabs[d].T
    wait_all(last)


def turn(where, activations, target, late):
    return local_call(
        turn_kernel,
        [((8, TOK, SLAB), BF16), ((8, SLAB, TOK), BF16), rows16(TOK)],
        [],
        [pltpu.SemaphoreType.DMA((9,))],
        [where],
        [],
        [activations, target],
        late,
    )


def share_kernel(mine, other, share):
    share[...] = add_rounded(mine[...], other[...])


def add_share(mine, other, late=()):
    return local_call(share_kernel, [rows16(FRAG // 2)], [], [], near=[mine, other], late=late)[0]


def share_first_kernel(held, mine, other, same, share):
    share[...] = add_rounded(mine[...], other[...])


def second_y_kernel(w_lo, back_hi, z_lo, mine, other, to_next, to_back, share):
    to_next[:HALF] = z_lo[...]
    to_next[HALF:] = back_hi[...]
    to_back[:HALF] = z_lo[...]
    to_back[HALF:] = w_lo[...]
    share[...] = add_rounded(mine[...], other[...])


def second_z_kernel(w_hi, back_hi, next_hi, to_z):
    to_z[:HALF] = w_hi[...]
    to_z[HALF : 2 * HALF] = next_hi[...]
    to_z[2 * HALF :] = back_hi[...]


def third_kernel(w_lo, y_back, y_next, mine, other, to_next, to_back, to_z, share):
    to_next[:PART] = y_back[PART:HALF]
    to_next[PART:] = w_lo[...]
    to_back[:PART] = y_next[:PART]
    to_back[PART:] = y_next[HALF:]
    to_z[...] = y_back[HALF:]
    share[...] = add_rounded(mine[...], other[...])


def parts_of(parts, sources):
    values = [sources[source][at : at + rows] for source, at, rows in parts]
    return values[0] if len(values) == 1 else jnp.concatenate(values, axis=0)


def value_terms(table, slabs, sources):
    for shard, row, parts in table:
        weights = parts_of(parts, sources)
        columns = slabs[AT[shard], :, row : row + weights.shape[0]]
        yield jnp.dot(columns, weights, preferred_element_type=F32)


def forward_kernel(table, slabs, *refs):
    *sources, out = refs
    for j, term in enumerate(value_terms(table, slabs, sources)):
        out[...] = term if j == 0 else out[...] + term


def forward(slabs, sources, table, late):
    kernel = functools.partial(forward_kernel, table)
    return local_call(kernel, [((TOK, HV), F32)], [], [], near=[slabs, *sources], late=late)[0]


def middle_kernel(table, slabs, turned, before, target, y_back, y_next, z_far, *outs):
    cot, to_next, to_back, to_z, p02_hi, p03_hi = outs
    total = before[...]
    for term in value_terms(table, slabs, (y_back, y_next, z_far)):
        total = total + term
    cot[...] = (total * SCALE - target[...].astype(F32)).astype(BF16)
    p12, p02, p03 = (
        jnp.dot(turned[d], cot[...], preferred_element_type=F32).astype(BF16) for d in range(3)
    )
    to_next[:SOME] = p12[:SOME]
    to_next[SOME:] = p02[:LOWER]
    to_back[:SOME] = p12[SOME:LOWER]
    to_back[SOME:] = p03[:LOWER]
    to_z[...] = p12[LOWER:]
    p02_hi[...] = p02[LOWER:]
    p03_hi[...] = p03[LOWER:]


def middle(slabs, turned, before, target, sources, table):
    three = [rows16(SOME + LOWER), rows16(SOME + LOWER), rows16(UPPER)]
    return local_call(
        functools.partial(middle_kernel, table),
        [rows16(TOK)] + three + [rows16(UPPER)] * 2,
        [],
        [],
        near=[slabs, turned, before, target, *sources],
    )


def backward_kernel(turned, cot, p11_lo, p13_lo, p10_lo, to_z, p01, p00):
    for i, low in enumerate((p11_lo, p13_lo, p10_lo)):
        part = jnp.dot(turned[3 + i], cot[...], preferred_element_type=F32).astype(BF16)
        low[...] = part[:LOWER]
        to_z[i * UPPER : (i + 1) * UPPER] = part[LOWER:]
    p01[...] = jnp.dot(turned[6], cot[...], preferred_element_type=F32).astype(BF16)
    p00[...] = jnp.dot(turned[7], cot[...], preferred_element_type=F32).astype(BF16)


def input_kernel(table, where, cot, *refs):
    *sources, out, products, sems = refs
    stores = []
    for j, (shard, parts) in enumerate(table):
        product = lax.dot_general(
            cot[...],
            parts_of(parts, sources),
            (((1,), (1,)), ((), ())),
            preferred_element_type=F32,
        )
        products[j] = (product * SCALE).astype(BF16)
        stores += start_all([(products.at[j], out.at[:, slab_columns(where, shard)])], sems, j)
    wait_all(stores)


def input_gradient(where, cotangent, sources, table, late):
    by_shard = [(d, sum([p for s, _, p in sorted(table, key=lambda t: t[1]) if s == d], [])) for d in ORDER[::-1]]
    return local_call(
        functools.partial(input_kernel, by_shard),
        [],
        [((TOK, DW), BF16)],
        [pltpu.VMEM((8, TOK, SLAB), BF16), pltpu.SemaphoreType.DMA((8,))],
        [where],
        [cotangent, *sources],
        [],
        late,
    )[0]


def join_second_a_kernel(p11_lo, p01, from_back, to_next):
    to_next[:SOME] = add_rounded(p11_lo[:SOME], from_back[:SOME])
    to_next[SOME:LOWER] = p11_lo[SOME:]
    to_next[LOWER:] = add_rounded(p01[:LOWER], from_back[SOME:])


def join_second_b_kernel(p13_lo, p02_hi, from_next, in02_hi, to_back):
    to_back[:SOME] = p13_lo[:SOME]
    to_back[SOME:LOWER] = add_rounded(p13_lo[SOME:], from_next[:SOME])
    to_back[LOWER:] = add_rounded(p02_hi[...], in02_hi[...])


def join_third_kernel(
    p01, p03_hi, p10_lo, from_back, from_next, in_hi, mine, other, to_next, to_back, to_z, share
):
    to_next[...] = add_rounded(p01[LOWER:], in_hi[:UPPER])
    to_back[...] = add_rounded(p03_hi[...], in_hi[UPPER : 2 * UPPER], from_next[LOWER:])
    to_z[...] = add_rounded(p10_lo[...], from_back[:LOWER], from_next[:LOWER])
    share[...] = add_rounded(mine[...], other[...])


def outer_kernel(plan, outer, moment, pending, params, inner, late, old, speed, new_outer, new_moment, held, push, came, sems):
    loads = start_all(
        [(outer, held), (moment, push), (pending, came), (params, old), (inner, speed)], sems
    )
    wait_all(loads[:3])
    rows = pl.ds(pl.multiple_of(plan[0] * FRAG, FRAG), FRAG)
    arrived = came[...]
    moment_late = OUTER_BETA * push[rows, :] + arrived
    outer_late = held[rows, :] - OUTER_RATE * (arrived + OUTER_BETA * moment_late)
    push[rows, :] = moment_late
    held[rows, :] = outer_late
    late[...] = outer_late
    stores = start_all([(held, new_outer), (push, new_moment)], sems, 5)
    wait_all(loads[3:] + stores)


def outer_step(plan, outer, moment, pending, params, inner, late):
    return local_call(
        outer_kernel,
        [((FRAG, HV), F32), ((SLAB, HV), F32), ((SLAB, HV), F32)],
        [((SLAB, HV), F32)] * 2,
        [
            pltpu.VMEM((SLAB, HV), F32),
            pltpu.VMEM((SLAB, HV), F32),
            pltpu.VMEM((FRAG, HV), F32),
            pltpu.SemaphoreType.DMA((7,)),
        ],
        [plan],
        [],
        [outer, moment, pending, params, inner],
        late,
    )


def step_kernel(where, plan, late, old, speed, share, other, own, low1, low2, low3, high1, high2, high3, *refs):
    new_params, new_moment, new_pending, params, moment, mean, sems = refs
    terms = [(low1, SOME), (low2, LOWER), (low3, 0)], [(high1, 2 * UPPER), (high2, 0), (high3, 0)]
    half = FRAG // 2
    mean[pl.ds(pl.multiple_of(where[1] * half, half), half), :] = share[...].astype(F32) / N_REP
    mean[pl.ds(pl.multiple_of((1 - where[1]) * half, half), half), :] = other[...].astype(F32) / N_REP
    stores = start_all([(mean, new_pending)], sems, 2 * NFRAG)
    for i in range(NFRAG):
        rows = pl.ds(i * FRAG, FRAG)
        first, end = i * FRAG, (i + 1) * FRAG
        cuts = [(0, first, min(end, LOWER)), (1, max(first, LOWER), end)]
        others = []
        for part, begin, stop in cuts:
            if begin < stop:
                at = begin - part * LOWER
                others.append(add16(*[t[row + at : row + at + stop - begin] for t, row in terms[part]]))
        others = others[0] if len(others) == 1 else jnp.concatenate(others, axis=0)
        fresh = INNER_BETA * speed[rows, :] + add16(own[rows, :], others) * SCALE
        moment[rows, :] = fresh
        stores += start_all([(moment.at[rows], new_moment.at[rows])], sems, 2 * i)
        stepped = old[rows, :] - INNER_RATE * fresh
        merged = MIX_SHARE * stepped + MIX_SHARE * late[...]
        params[rows, :] = jnp.where(plan[0] == i, merged, stepped)
        stores += start_all([(params.at[rows], new_params.at[rows])], sems, 2 * i + 1)
    wait_all(stores)


def inner_step(where, plan, near):
    return local_call(
        step_kernel,
        [],
        [((SLAB, HV), F32), ((SLAB, HV), F32), ((FRAG, HV), F32)],
        [
            pltpu.VMEM((SLAB, HV), F32),
            pltpu.VMEM((SLAB, HV), F32),
            pltpu.VMEM((FRAG, HV), F32),
            pltpu.SemaphoreType.DMA((2 * NFRAG + 1,)),
        ],
        [where, plan],
        near,
    )


def body(activations, target, params, momentum, outer_params, outer_momentum, pending, plan):
    weights, moment = params[0], momentum[0]
    where = jnp.stack([lax.axis_index("fsdp"), lax.axis_index("rep") % 2]).astype(jnp.int32)
    share_rows = rows16(FRAG // 2)

    w, w_lo, w_hi = first(weights)
    z_lo, back_hi, next_hi = move_z(w_lo), move_y(w_hi, 1), move_y(w_hi, -1)
    mine, theirs = leaving(where, plan, weights, outer_params, [(w, False)])
    other = swap_core(theirs)

    to_next, to_back, share = local_call(
        second_y_kernel,
        [rows16(2 * HALF), rows16(2 * HALF), share_rows],
        [],
        [],
        near=[w_lo, back_hi, z_lo, mine, other],
    )
    to_z = local_call(
        second_z_kernel, [rows16(3 * HALF)], [], [], near=[w_hi, back_hi, next_hi]
    )[0]
    z_hi, y_back, y_next = move_z(to_z), move_y(to_next, 1), move_y(to_back, -1)
    slabs, turned, goal = turn(where, activations, target, [(share, False)])
    share = add_share(share, swap_x(share, 1))
    other = swap_x(share, 3)

    to_next, to_back, to_z, share = local_call(
        third_kernel,
        [rows16(PART + HALF), rows16(PART + HALF), rows16(HALF), share_rows],
        [],
        [],
        near=[w_lo, y_back, y_next, share, other],
        late=[(goal, False)],
    )
    z_far, y_back3, y_next3 = move_z(to_z), move_y(to_next, 1), move_y(to_back, -1)
    other = swap_z(share, 1)

    near = [w, next_hi, back_hi, z_lo, y_back, y_next, z_hi]
    upper = SLAB - HALF
    table = [
        (0, 0, [(0, 0, SLAB)]),
        (1, 0, [(5, HALF, HALF), (1, 0, upper)]),
        (4, 0, [(3, 0, HALF), (6, 0, upper)]),
        (5, 0, [(5, 0, HALF), (6, HALF, upper)]),
        (7, 0, [(4, 0, HALF), (6, 2 * HALF, upper)]),
        (3, HALF, [(2, 0, upper)]),
        (2, HALF, [(4, HALF, upper)]),
    ]
    late, old, speed, new_outer, new_outer_momentum = outer_step(
        plan, outer_params, outer_momentum, pending, weights, moment, [(to_z, False)]
    )
    values = forward(slabs, near, table, [(late, False)])
    last = [y_back3, y_next3, z_far]
    cotangent, to_next, to_back, to_z, p02_hi, p03_hi = middle(
        slabs,
        turned,
        values,
        goal,
        last,
        [
            (3, 0, [(0, PART, HALF)]),
            (2, 0, [(1, PART, HALF)]),
            (6, 0, [(1, 0, PART), (0, 0, PART), (2, 0, upper)]),
        ],
    )

    in02_hi, from_back, from_next = move_z(to_z), move_y(to_next, 1), move_y(to_back, -1)
    low1 = from_next
    p11_lo, p13_lo, p10_lo, to_z, p01, p00 = local_call(
        backward_kernel,
        [rows16(LOWER)] * 3 + [rows16(3 * UPPER), rows16(SLAB), rows16(SLAB)],
        [],
        [],
        near=[turned, cotangent],
    )
    to_z, share = local_call(
        share_first_kernel,
        [rows16(3 * UPPER), share_rows],
        [],
        [],
        near=[to_z, share, other],
        aliases={0: 0},
    )
    in_hi = move_z(to_z)

    to_next = local_call(
        join_second_a_kernel, [rows16(2 * LOWER)], [], [], near=[p11_lo, p01, from_back]
    )[0]
    to_back = local_call(
        join_second_b_kernel,
        [rows16(SLAB)],
        [],
        [],
        near=[p13_lo, p02_hi, from_next, in02_hi],
        late=[(to_next, False)],
    )[0]
    from_back, from_next = move_y(to_next, 1), move_y(to_back, -1)
    low2 = from_back
    other = swap_z(share, 3)
    table += [
        (3, 0, [(7, PART, HALF)]),
        (2, 0, [(8, PART, HALF)]),
        (6, 0, [(8, 0, PART), (7, 0, PART), (9, 0, upper)]),
    ]
    grad_input = input_gradient(where, cotangent, near + last, table, [(to_back, False)])

    to_next, to_back, to_z, share = local_call(
        join_third_kernel,
        [rows16(UPPER), rows16(UPPER), rows16(LOWER), share_rows],
        [],
        [],
        near=[p01, p03_hi, p10_lo, from_back, from_next, in_hi, share, other],
        late=[(grad_input, True)],
    )
    low3, high2, high3 = move_z(to_z), move_y(to_next, 1), move_y(to_back, -1)
    other = swap_core(share)

    terms = [p00, low1, low2, low3, in_hi, high2, high3]
    new_params, new_moment, new_pending = inner_step(
        where, plan, [late, old, speed, share, other, *terms]
    )
    return (
        new_params[None],
        new_moment[None],
        grad_input,
        new_outer,
        new_outer_momentum,
        new_pending,
    )


def solution(mesh):
    placed = (
        P(("rep", "fsdp"), None),
        P(("rep", "fsdp"), None),
        P("rep", "fsdp", None),
        P("rep", "fsdp", None),
        P("fsdp", None),
        P("fsdp", None),
        P("fsdp", None),
        P(),
    )
    return jax.shard_map(
        body,
        mesh=mesh,
        in_specs=placed,
        out_specs=(
            P("rep", "fsdp", None),
            P("rep", "fsdp", None),
            P(("rep", "fsdp"), None),
            P("fsdp", None),
            P("fsdp", None),
            P("fsdp", None),
        ),
        check_vma=False,
    )
```
